512 devices in a mesh: dom: 64 (over z_lo, x, y), rep: 8 (over z_hi, core).
Axes of the slice: x: 4, y: 8, z: 8 (z_hi: 4, z_lo: 2; z = z_hi * 2 + z_lo), core: 2. Of those that a mesh axis runs over, the one named last changes fastest.
Arguments:
- features: bfloat16 [32768, 256], P('dom'), may hold values from -6 to 6
- weight: bfloat16 [256, 256], replicated, may hold values from -0.375 to 0.375
- grad_out: bfloat16 [32768, 256], P('dom'), may hold values from -6 to 6
- tiles: bfloat16 [64, 64, 512, 512], P('dom', 'rep'), may hold values from -0.125 to 0.125
- tile_mask: int32 [64, 64], P('dom', 'rep'), may hold values from 0 to 1, as said below
Outputs:
- activated: bfloat16 [32768, 256], P('dom')
- feature_grad: bfloat16 [32768, 256], P('dom')
- weight_grad: float32 [256, 256], replicated
The draws below stay inside these ranges and needn't reach their ends.
Inputs may be any that keep to these rules, and one draw needn't show every extreme that they name: `tile_mask`: the diagonal tiles (offset 0) are always present; other tiles are sparse, more frequent near the diagonal (small offsets or offsets near 64), and some row blocks hold many more tiles than others.
All inputs are finite; a program needn't handle non-finite values.
Results may differ from the reference program's by a relative error of at most 0.007.
Values may be sent and summed in bfloat16 or wider, within the bound.
No kernel may reach another device: no remote copies, remote signals or barrier semaphores. Data moves between devices by JAX's collectives and lax.ppermute only.
A program may use at most 64 MiB of HBM per device.

```python
import jax
import jax.numpy as jnp
from jax import lax

ROWS_DEV = 512
HIDDEN_SIZE = 256
BLOCKS = 64
NODES = 32768


def draw_tile_mask(key, part):
    key = jax.random.fold_in(key, 11)
    heavy_key, roll_key = jax.random.split(key)
    offsets = jnp.arange(BLOCKS, dtype=jnp.int32)
    distance = jnp.minimum(offsets, BLOCKS - offsets)
    safe_distance = jnp.maximum(distance, 1)
    chance = 500 // (safe_distance * safe_distance) + 40
    heavy = jnp.where(jax.random.randint(heavy_key, (BLOCKS, 1), 0, 4) == 0, 3, 1).astype(jnp.int32)
    roll = jax.random.randint(roll_key, (BLOCKS, BLOCKS), 0, 1000)
    present = (roll < chance[None, :] * heavy).astype(jnp.int32)
    return jnp.where(distance[None, :] == 0, 1, present).astype(jnp.int32)


def level_of(key, dims, shards, least, largest):
    gain, own = 1.0, jax.random.fold_in(key, 6)
    for position, shards_of in shards:
        heights = jnp.exp(jax.random.uniform(jax.random.fold_in(own, position), (shards_of,), jnp.float32, least / len(shards), largest / len(shards)))
        gain = gain * jnp.repeat(heights, dims[position] // shards_of).reshape([-1 if axis == position else 1 for axis in range(len(dims))])
    return gain


def bell_draw(stream_key, dims, deviation, bound, pieces=(), kind=jnp.bfloat16):
    entries = deviation * jax.random.normal(stream_key, dims, jnp.float32)
    if pieces:
        entries = entries * level_of(stream_key, dims, pieces, -0.22, 0.18)
    return jnp.clip(entries, -bound, bound).astype(kind)


def setup_inputs(seed: int = 0) -> dict:
    key_list = jax.random.split(jax.random.key(seed), 6)
    features = bell_draw(key_list[0], (NODES, HIDDEN_SIZE), 1.0, 6.0, ((0, 64),))
    weight = bell_draw(key_list[1], (HIDDEN_SIZE, HIDDEN_SIZE), HIDDEN_SIZE ** -0.5, 0.375)
    grad_out = bell_draw(key_list[2], (NODES, HIDDEN_SIZE), 1.0, 6.0, ((0, 64),))
    tiles = bell_draw(key_list[3], (BLOCKS, BLOCKS, ROWS_DEV, ROWS_DEV), (4 * ROWS_DEV) ** -0.5, 0.125, ((0, 64), (1, 8)))
    tile_mask = draw_tile_mask(jax.random.fold_in(key_list[5], 71), 0)
    return {"features": features, "weight": weight, "grad_out": grad_out, "tiles": tiles, "tile_mask": tile_mask}


def reference(features, weight, grad_out, tiles, tile_mask):
    projected = jnp.dot(features, weight, preferred_element_type=jnp.float32).astype(jnp.bfloat16)
    blocks = projected.reshape(BLOCKS, ROWS_DEV, HIDDEN_SIZE)
    offsets = jnp.arange(BLOCKS, dtype=jnp.int32)

    def row_sum(i):
        columns = ((i - offsets) % BLOCKS).astype(jnp.int32)
        weight_flag = tile_mask[i].astype(jnp.float32)
        tile_block = tiles[i].astype(jnp.float32) * weight_flag[:, None, None]
        return jnp.einsum('orc,ocf->rf', tile_block, blocks[columns].astype(jnp.float32))

    total = lax.map(row_sum, offsets).reshape(NODES, HIDDEN_SIZE)
    gate_value = jax.nn.sigmoid(total)
    activated = (total * gate_value).astype(jnp.bfloat16)
    score_grad = (grad_out.astype(jnp.float32) * gate_value * (1.0 + total * (1.0 - gate_value))).astype(jnp.bfloat16)
    score_blocks = score_grad.reshape(BLOCKS, ROWS_DEV, HIDDEN_SIZE)

    def column_sum(j):
        row_ids = ((j + offsets) % BLOCKS).astype(jnp.int32)
        weight_flag = tile_mask[row_ids, offsets].astype(jnp.float32)
        tile_block = tiles[row_ids, offsets].astype(jnp.float32) * weight_flag[:, None, None]
        return jnp.einsum('orc,orf->cf', tile_block, score_blocks[row_ids].astype(jnp.float32))

    node_grad = lax.map(column_sum, offsets).reshape(NODES, HIDDEN_SIZE).astype(jnp.bfloat16)
    feature_grad = jnp.dot(node_grad, weight.T, preferred_element_type=jnp.float32).astype(jnp.bfloat16)
    weight_grad = jnp.dot(features.T, node_grad, preferred_element_type=jnp.float32) * (NODES ** -0.5)
    return activated, feature_grad, weight_grad
```

```python
import functools

import jax
import jax.numpy as jnp
from jax import lax
from jax.experimental import pallas as pl
from jax.experimental.pallas import tpu as pltpu
from jax.sharding import Mesh
from jax.sharding import PartitionSpec as P

AXES = ("zl", "x", "y", "zh", "c")
SIZES = (2, 4, 8, 4, 2)
DOM = ("zl", "x", "y")
BLOCKS = 64
REPLICAS = 8
ROWS = 512
HALF = 256
HIDDEN = 256
F32 = jnp.float32
BF16 = jnp.bfloat16
SMEM = pl.BlockSpec(memory_space=pltpu.SMEM)
VMEM = pl.BlockSpec(memory_space=pltpu.VMEM)
ANY = pl.BlockSpec(memory_space=pl.ANY)
PARAMS = pltpu.CompilerParams(vmem_limit_bytes=40 * 1024 * 1024)


def route(value, target):
    pairs = []
    for i in range(BLOCKS):
        for r in range(REPLICAS):
            i2, r2 = target(i, r)
            pairs.append((i * REPLICAS + r, (i2 % BLOCKS) * REPLICAS + r2 % REPLICAS))
    return lax.ppermute(value, AXES, pairs)


def first_of(r):
    return 4 * (r % 2)


def partner(i, r):
    return (i + 8, r + 1) if r % 2 == 0 else (i - 8, r - 1)


def swap_pair(value):
    return route(value, partner)


def swap_core(value):
    return lax.ppermute(value, "c", [(0, 1), (1, 0)])


def start_tiles(mask_ref, tiles_ref, held, sems, indices):
    for t in indices:

        @pl.when(mask_ref[0, t] > 0)
        def _():
            pltpu.make_async_copy(tiles_ref.at[0, t], held.at[t], sems.at[t]).start()


def wait_tile(tiles_ref, held, sems, t):
    pltpu.make_async_copy(tiles_ref.at[0, t], held.at[t], sems.at[t]).wait()


def forward_kernel(core_ref, mask_ref, tiles_ref, g0, g1, g2, g3, e12, e03, keep_ref, send_ref, held, acc, sems):
    core = core_ref[0]
    mine, other = core * 4, 4 - core * 4
    order = [
        (mine + 1, g1, 0),
        (mine + 2, g2, 0),
        (mine, g0, 0),
        (mine + 3, g3, 0),
        (other + 1, e12, 0),
        (other + 2, e12, ROWS),
        (other, e03, 0),
        (other + 3, e03, ROWS),
    ]
    start_tiles(mask_ref, tiles_ref, held, sems, [t for t, _, _ in order])
    acc[...] = jnp.zeros_like(acc)
    for t, block, start in order:

        @pl.when(mask_ref[0, t] > 0)
        def _():
            wait_tile(tiles_ref, held, sems, t)
            acc[...] += jnp.dot(held[t], block[start : start + ROWS, :], preferred_element_type=F32)

    keep_ref[...] = acc[pl.ds(pl.multiple_of(core * HALF, HALF), HALF), :]
    send_ref[...] = acc[pl.ds(pl.multiple_of(HALF - core * HALF, HALF), HALF), :]


def middle_kernel(zh_ref, parts_ref, weight_ref, grad_ref, pack_ref, term_ref, full):
    wide = parts_ref[0].astype(F32)
    for s in range(1, 4):
        wide = wide + parts_ref[s].astype(F32)
    high = wide.astype(BF16)
    low = (wide - high.astype(F32)).astype(BF16)
    weight = weight_ref[...]
    total = jnp.dot(high, weight, preferred_element_type=F32) + jnp.dot(low, weight, preferred_element_type=F32)
    gate = jax.nn.sigmoid(total)
    pack_ref[0] = (total * gate).astype(BF16)
    score = (grad_ref[...].astype(F32) * gate * (1.0 + total * (1.0 - gate))).astype(BF16)
    pack_ref[1] = lax.dot_general(weight, score, (((1,), (1,)), ((), ())), preferred_element_type=F32).astype(BF16)
    full[...] = lax.dot_general(high, score, (((0,), (0,)), ((), ())), preferred_element_type=F32)
    term_ref[...] = full[pl.ds(pl.multiple_of(zh_ref[0] * 64, 64), 64), :]


def backward_kernel(plan, core_ref, mask_ref, tiles_ref, pack_ref, *rest):
    outs, held, sems = rest[: len(plan)], rest[-2], rest[-1]
    core = core_ref[0]
    base = (core * 4, 4 - core * 4)
    work = [(base[side] + q, out, slot) for out, entries in zip(outs, plan) for slot, (side, q) in enumerate(entries)]
    start_tiles(mask_ref, tiles_ref, held, sems, [t for t, _, _ in work])
    for t, out, slot in work:

        @pl.when(mask_ref[0, t] > 0)
        def _():
            wait_tile(tiles_ref, held, sems, t)
            value = jnp.dot(pack_ref[0, 1], held[t, :HALF, :], preferred_element_type=F32)
            value = value + jnp.dot(pack_ref[1, 1], held[t, HALF:, :], preferred_element_type=F32)
            value = value.astype(BF16)
            out[slot, 0] = value[:, :HALF]
            out[slot, 1] = value[:, HALF:]

        @pl.when(mask_ref[0, t] == 0)
        def _():
            out[slot] = jnp.zeros((2, HIDDEN, HALF), BF16)


def last_kernel(parts_ref, out_ref):
    wide = parts_ref[0].astype(F32)
    for s in range(1, 4):
        wide = wide + parts_ref[s].astype(F32)
    out_ref[...] = wide.T.astype(BF16)


def products(plan, core, mask, tiles, pack):
    return pl.pallas_call(
        functools.partial(backward_kernel, plan),
        out_shape=[jax.ShapeDtypeStruct((len(entries), 2, HIDDEN, HALF), BF16) for entries in plan],
        in_specs=[SMEM, SMEM, ANY, VMEM],
        out_specs=[VMEM] * len(plan),
        scratch_shapes=[pltpu.VMEM((8, ROWS, ROWS), BF16), pltpu.SemaphoreType.DMA((8,))],
        compiler_params=PARAMS,
        cost_estimate=pl.CostEstimate(flops=10**9, bytes_accessed=6 * 2**20, transcendentals=0),
    )(core, mask, tiles, pack)


def total_of(*values):
    wide = values[0].astype(F32)
    for value in values[1:]:
        wide = wide + value.astype(F32)
    return wide


def shards(features, weight, grad_out, tiles, tile_mask):
    core_index = lax.axis_index("c")
    core = core_index.astype(jnp.int32).reshape(1)
    zh = lax.axis_index("zh").astype(jnp.int32).reshape(1)

    g1 = route(features, lambda i, r: (i + 8 * r + first_of(r) + 1, r))
    g2 = route(features, lambda i, r: (i + 8 * r + first_of(r) + 2, r))
    g0 = route(g1, lambda i, r: (i - 1, r))
    g3 = route(g2, lambda i, r: (i + 1, r))
    e12 = swap_pair(jnp.concatenate([g1, g2]))
    e03 = swap_pair(jnp.concatenate([g0, g3]))
    half = jax.ShapeDtypeStruct((HALF, HIDDEN), F32)
    keep, send = pl.pallas_call(
        forward_kernel,
        out_shape=[half, half],
        in_specs=[SMEM, SMEM, ANY] + [VMEM] * 6,
        out_specs=[VMEM, VMEM],
        scratch_shapes=[
            pltpu.VMEM((8, ROWS, ROWS), BF16),
            pltpu.VMEM((ROWS, HIDDEN), F32),
            pltpu.SemaphoreType.DMA((8,)),
        ],
        compiler_params=PARAMS,
        cost_estimate=pl.CostEstimate(flops=10**9, bytes_accessed=6 * 2**20, transcendentals=0),
    )(core, tile_mask, tiles, g0, g1, g2, g3, e12, e03)
    chip = (keep + swap_core(send)).astype(BF16)
    parts = lax.all_gather(chip, "zh")
    grad_half = lax.dynamic_slice_in_dim(grad_out, core_index * HALF, HALF, 0)
    pack, term = pl.pallas_call(
        middle_kernel,
        out_shape=[
            jax.ShapeDtypeStruct((2, HALF, HIDDEN), BF16),
            jax.ShapeDtypeStruct((64, HIDDEN), F32),
        ],
        in_specs=[SMEM] + [VMEM] * 3,
        out_specs=[VMEM, VMEM],
        scratch_shapes=[pltpu.VMEM((HIDDEN, HIDDEN), F32)],
        compiler_params=PARAMS,
    )(zh, parts, weight, grad_half)
    packs = lax.all_gather(pack, "c")
    activated = packs[:, 0].reshape(ROWS, HIDDEN)

    (send03,) = products((((1, 0), (1, 3)),), core, tile_mask, tiles, packs)
    r03 = swap_pair(send03)
    send12, own = products((((1, 1), (1, 2)), ((0, 0), (0, 1), (0, 2), (0, 3))), core, tile_mask, tiles, packs)
    r12 = swap_pair(send12)
    n0 = total_of(own[0], r03[0]).astype(BF16)
    n3 = total_of(own[3], r03[1]).astype(BF16)
    t0 = route(n0, lambda i, r: (i + 1, r))
    t3 = route(n3, lambda i, r: (i - 1, r))
    n1 = total_of(own[1], r12[0], t0).astype(BF16)
    n2 = total_of(own[2], r12[1], t3).astype(BF16)
    d1 = route(n1, lambda i, r: (i - 8 * r - first_of(r) - 1, r))
    d2 = route(n2, lambda i, r: (i - 8 * r - first_of(r) - 2, r))
    both = total_of(d1, d2)
    flipped = jnp.where(core_index == 0, both[1], both[0])
    kept = jnp.where(core_index == 0, both[0], both[1])
    chip_grad = (kept + swap_core(flipped)).astype(BF16)
    grad_parts = lax.all_gather(chip_grad, "zh")
    grad_rows = pl.pallas_call(
        last_kernel,
        out_shape=jax.ShapeDtypeStruct((HALF, HIDDEN), BF16),
        in_specs=[VMEM],
        out_specs=VMEM,
        compiler_params=PARAMS,
    )(grad_parts)
    feature_grad = lax.all_gather(grad_rows, "c").reshape(ROWS, HIDDEN)

    spread = lax.all_to_all(term.reshape(BLOCKS, 1, HIDDEN), DOM, 0, 0)
    row = jnp.sum(spread, axis=0)
    row = (row + swap_core(row)) * (BLOCKS * ROWS) ** -0.5
    rows = lax.all_to_all(jnp.broadcast_to(row, (256, 1, HIDDEN)), ("zh",) + DOM, 0, 0)
    return activated, feature_grad, rows.reshape(HIDDEN, HIDDEN)


def solution(mesh):
    fine = Mesh(mesh.devices.reshape(SIZES), AXES)
    nodes = P(DOM, None)
    return jax.shard_map(
        shards,
        mesh=fine,
        in_specs=(nodes, P(), nodes, P(DOM, ("zh", "c"), None, None), P(DOM, ("zh", "c"))),
        out_specs=(nodes, nodes, P()),
        check_vma=False,
    )
```

```python
import functools

import jax
import jax.numpy as jnp
from jax import lax
from jax.experimental import pallas as pl
from jax.experimental.pallas import tpu as pltpu
from jax.sharding import Mesh
from jax.sharding import PartitionSpec as P

AXES = ("zl", "x", "y", "zh", "c")
SIZES = (2, 4, 8, 4, 2)
DOM = ("zl", "x", "y")
BLOCKS = 64
REPLICAS = 8
ROWS = 512
HALF = 256
HIDDEN = 256
F32 = jnp.float32
BF16 = jnp.bfloat16
SMEM = pl.BlockSpec(memory_space=pltpu.SMEM)
VMEM = pl.BlockSpec(memory_space=pltpu.VMEM)
HBM = pl.BlockSpec(memory_space=pltpu.HBM)
PARAMS = pltpu.CompilerParams(vmem_limit_bytes=24 * 1024 * 1024)
WIDE_PARAMS = pltpu.CompilerParams(vmem_limit_bytes=60 * 1024 * 1024)


def route(value, target):
    pairs = []
    for i in range(BLOCKS):
        for r in range(REPLICAS):
            i2, r2 = target(i, r)
            pairs.append((i * REPLICAS + r, (i2 % BLOCKS) * REPLICAS + r2 % REPLICAS))
    return lax.ppermute(value, AXES, pairs)


def partner(i, r):
    return (i + 8, r + 1) if r % 2 == 0 else (i - 8, r - 1)


def swap_pair(value):
    return route(value, partner)


def side(r):
    return 1 - 2 * (r % 2)


def offsets_of(core, pair, slot):
    return (7 * core, 1 + 5 * core, 2 + 3 * core, 3 + core)[2 * pair + slot]


def load_kernel(mask_ref, tiles_ref, held_ref, sems):
    def copy(t):
        return pltpu.make_async_copy(tiles_ref.at[0, t], held_ref.at[t], sems.at[t])

    for t in range(8):

        @pl.when(mask_ref[0, t] > 0)
        def _():
            copy(t).start()

    for t in range(8):

        @pl.when(mask_ref[0, t] > 0)
        def _():
            copy(t).wait()


def tile_steps(core_ref, mask_ref, held, work, present, absent):
    core = core_ref[0]
    for step, (member, pair, slot) in enumerate(work):
        t = offsets_of(core if member == 0 else 1 - core, pair, slot)

        @pl.when(mask_ref[0, t] > 0)
        def _():
            present(step, held.at[t])

        if absent is not None:

            @pl.when(mask_ref[0, t] == 0)
            def _():
                absent(step)


def early_kernel(core_ref, mask_ref, held, own0, other0, own1, acc):
    blocks = (own0, other0, own1)
    acc[...] = jnp.zeros_like(acc)

    def present(step, tile):
        start = (step % 2) * ROWS
        acc[...] += jnp.dot(tile[...], blocks[step // 2][start : start + ROWS, :], preferred_element_type=F32)

    work = [(member, pair, slot) for member, pair in ((0, 0), (1, 0), (0, 1)) for slot in range(2)]
    tile_steps(core_ref, mask_ref, held, work, present, None)


def late_kernel(core_ref, mask_ref, held, before, other1, keep_ref, send_ref, acc):
    core = core_ref[0]
    acc[...] = before[...]

    def present(step, tile):
        acc[...] += jnp.dot(tile[...], other1[step * ROWS : (step + 1) * ROWS, :], preferred_element_type=F32)

    tile_steps(core_ref, mask_ref, held, [(1, 1, 0), (1, 1, 1)], present, None)
    keep_ref[...] = acc[pl.ds(pl.multiple_of(core * HALF, HALF), HALF), :]
    send_ref[...] = acc[pl.ds(pl.multiple_of(HALF - core * HALF, HALF), HALF), :]


def middle_kernel(zh_ref, parts_ref, weight_ref, grad_ref, pack_ref, full):
    wide = parts_ref[0].astype(F32)
    for s in range(1, 4):
        wide = wide + parts_ref[s].astype(F32)
    high = wide.astype(BF16)
    low = (wide - high.astype(F32)).astype(BF16)
    weight = weight_ref[...]
    total = jnp.dot(high, weight, preferred_element_type=F32) + jnp.dot(low, weight, preferred_element_type=F32)
    gate = jax.nn.sigmoid(total)
    pack_ref[:HALF] = (total * gate).astype(BF16)
    score = (grad_ref[...].astype(F32) * gate * (1.0 + total * (1.0 - gate))).astype(BF16)
    turned = lax.dot_general(weight, score, (((1,), (1,)), ((), ())), preferred_element_type=F32)
    pack_ref[HALF : 2 * HALF] = turned.astype(BF16)
    full[...] = lax.dot_general(high, score, (((0,), (0,)), ((), ())), preferred_element_type=F32)
    term = full[pl.ds(pl.multiple_of(zh_ref[0] * 64, 64), 64), :]
    term_high = term.astype(BF16)
    pack_ref[512:576] = term_high
    pack_ref[576:640] = (term - term_high.astype(F32)).astype(BF16)


def backward_kernel(plan, core_ref, mask_ref, held, pack_ref, *outs):
    def present(step, tile):
        value = jnp.dot(pack_ref[0, HALF : 2 * HALF], tile[:HALF, :], preferred_element_type=F32)
        value = value + jnp.dot(pack_ref[1, HALF : 2 * HALF], tile[HALF:, :], preferred_element_type=F32)
        value = value.astype(BF16)
        outs[step // 2][step % 2, 0] = value[:, :HALF]
        outs[step // 2][step % 2, 1] = value[:, HALF:]

    def absent(step):
        outs[step // 2][step % 2] = jnp.zeros((2, HIDDEN, HALF), BF16)

    work = [(member, pair, slot) for member, pair in plan for slot in range(2)]
    tile_steps(core_ref, mask_ref, held, work, present, absent)


def turn_kernel(parts_ref, out_ref):
    wide = parts_ref[0, :HALF].astype(F32)
    for s in range(1, 4):
        wide = wide + parts_ref[s, :HALF].astype(F32)
    out_ref[:HALF] = wide.T.astype(BF16)
    for s in range(4):
        out_ref[HALF + 32 * s : HALF + 32 * (s + 1)] = parts_ref[s, HALF:]


def last_kernel(packs_ref, rows_ref, weight_ref):
    for c in range(2):
        rows_ref[c * HALF : (c + 1) * HALF] = packs_ref[c, :HALF]
        for s in range(4):
            start = HALF + 32 * s
            weight_ref[64 * s + 32 * c : 64 * s + 32 * c + 32] = packs_ref[c, start : start + 32].astype(F32)


def products(plan, core, mask, held, packs):
    return pl.pallas_call(
        functools.partial(backward_kernel, plan),
        out_shape=[jax.ShapeDtypeStruct((2, 2, HIDDEN, HALF), BF16) for _ in plan],
        in_specs=[SMEM, SMEM, VMEM, VMEM],
        out_specs=[VMEM] * len(plan),
        compiler_params=PARAMS,
        cost_estimate=pl.CostEstimate(flops=2 * 10**9, bytes_accessed=6 * 2**20, transcendentals=0),
    )(core, mask, held, packs)


def total_of(*values):
    wide = values[0].astype(F32)
    for value in values[1:]:
        wide = wide + value.astype(F32)
    return wide


def spread_sum(value, axes):
    copies = jnp.broadcast_to(value, (8,) + value.shape)
    return jnp.sum(lax.all_to_all(copies, axes, 0, 0), axis=0)


def shards(features, weight, grad_out, tiles, tile_mask):
    core_index = lax.axis_index("c")
    core = core_index.astype(jnp.int32).reshape(1)
    zh = lax.axis_index("zh").astype(jnp.int32).reshape(1)
    even = core_index == 0

    held = pl.pallas_call(
        load_kernel,
        out_shape=jax.ShapeDtypeStruct((8, ROWS, ROWS), BF16),
        in_specs=[SMEM, HBM],
        out_specs=VMEM,
        scratch_shapes=[pltpu.SemaphoreType.DMA((8,))],
        compiler_params=WIDE_PARAMS,
    )(tile_mask, tiles)
    fetched1 = route(features, lambda i, r: (i + 8 * r + 2 + 3 * (r % 2), r))
    fetched0 = route(features, lambda i, r: (i + 8 * r + 7 * (r % 2), r))
    own0 = jnp.concatenate([fetched0, route(fetched0, lambda i, r: (i + side(r), r))])
    own1 = jnp.concatenate([fetched1, route(fetched1, lambda i, r: (i + side(r), r))])
    other0 = swap_pair(own0)
    other1 = swap_pair(own1)
    half = jax.ShapeDtypeStruct((HALF, HIDDEN), F32)
    before = pl.pallas_call(
        early_kernel,
        out_shape=jax.ShapeDtypeStruct((ROWS, HIDDEN), F32),
        in_specs=[SMEM, SMEM] + [VMEM] * 4,
        out_specs=VMEM,
        compiler_params=PARAMS,
        cost_estimate=pl.CostEstimate(flops=2 * 10**9, bytes_accessed=6 * 2**20, transcendentals=0),
    )(core, tile_mask, held, own0, other0, own1)
    keep, send = pl.pallas_call(
        late_kernel,
        out_shape=[half, half],
        in_specs=[SMEM, SMEM] + [VMEM] * 3,
        out_specs=[VMEM, VMEM],
        scratch_shapes=[pltpu.VMEM((ROWS, HIDDEN), F32)],
        compiler_params=PARAMS,
    )(core, tile_mask, held, before, other1)
    sent = lax.all_gather(send, "c")
    chip = (keep + jnp.where(even, sent[1], sent[0])).astype(BF16)
    parts = lax.all_gather(chip, "zh")
    grad_half = lax.dynamic_slice_in_dim(grad_out, core_index * HALF, HALF, 0)
    pack = pl.pallas_call(
        middle_kernel,
        out_shape=jax.ShapeDtypeStruct((640, HIDDEN), BF16),
        in_specs=[SMEM] + [VMEM] * 3,
        out_specs=VMEM,
        scratch_shapes=[pltpu.VMEM((HIDDEN, HIDDEN), F32)],
        compiler_params=PARAMS,
    )(zh, parts, weight, grad_half)
    packs = lax.all_gather(pack, "c")
    activated = packs[:, :HALF].reshape(ROWS, HIDDEN)

    (send1,) = products(((1, 1),), core, tile_mask, held, packs)
    got1 = swap_pair(send1)
    send0, mine0, mine1 = products(((1, 0), (0, 0), (0, 1)), core, tile_mask, held, packs)
    got0 = swap_pair(send0)
    back1 = route(total_of(mine1[1], got1[1]).astype(BF16), lambda i, r: (i - side(r), r))
    back0 = route(total_of(mine0[1], got0[1]).astype(BF16), lambda i, r: (i - side(r), r))
    far = total_of(mine1[0], got1[0], back1).astype(BF16)
    home_far = route(far, lambda i, r: (i - 8 * r - 2 - 3 * (r % 2), r))
    near = total_of(mine0[0], got0[0], back0).astype(BF16)
    home_near = route(near, lambda i, r: (i - 8 * r - 7 * (r % 2), r))

    high, low = packs[:, 512:576].astype(F32), packs[:, 576:640].astype(F32)
    term = lax.dynamic_slice_in_dim(high[0] + low[0] + (high[1] + low[1]), core_index * 32, 32, 0)
    term = spread_sum(term, "y")
    term, _ = lax.optimization_barrier((term, far))
    term = (spread_sum(term, ("zl", "x")) * (BLOCKS * ROWS) ** -0.5).astype(BF16)

    flipped = total_of(jnp.where(even, home_near[1], home_near[0]), jnp.where(even, home_far[1], home_far[0]))
    kept = total_of(jnp.where(even, home_near[0], home_near[1]), jnp.where(even, home_far[0], home_far[1]))
    crossed = lax.all_gather(flipped, "c")
    chip_grad = (kept + jnp.where(even, crossed[1], crossed[0])).astype(BF16)
    grad_parts = lax.all_gather(jnp.concatenate([chip_grad, term]), "zh")
    turned = pl.pallas_call(
        turn_kernel,
        out_shape=jax.ShapeDtypeStruct((HALF + 128, HIDDEN), BF16),
        in_specs=[VMEM],
        out_specs=VMEM,
        compiler_params=PARAMS,
    )(grad_parts)
    feature_grad, weight_grad = pl.pallas_call(
        last_kernel,
        out_shape=[jax.ShapeDtypeStruct((ROWS, HIDDEN), BF16), jax.ShapeDtypeStruct((HIDDEN, HIDDEN), F32)],
        in_specs=[VMEM],
        out_specs=[VMEM, VMEM],
        compiler_params=PARAMS,
    )(lax.all_gather(turned, "c"))
    return activated, feature_grad, weight_grad


def solution(mesh):
    fine = Mesh(mesh.devices.reshape(SIZES), AXES)
    nodes = P(DOM, None)
    return jax.shard_map(
        shards,
        mesh=fine,
        in_specs=(nodes, P(), nodes, P(DOM, ("zh", "c"), None, None), P(DOM, ("zh", "c"))),
        out_specs=(nodes, nodes, P()),
        check_vma=False,
    )
```

```python
import functools

import jax
import jax.numpy as jnp
from jax import lax
from jax.experimental import pallas as pl
from jax.experimental.pallas import tpu as pltpu
from jax.sharding import Mesh
from jax.sharding import PartitionSpec as P

AXES = ("zl", "x", "y", "zh", "c")
SIZES = (2, 4, 8, 4, 2)
DOM = ("zl", "x", "y")
BLOCKS = 64
REPLICAS = 8
ROWS = 512
HALF = 256
HIDDEN = 256
F32 = jnp.float32
BF16 = jnp.bfloat16
SMEM = pl.BlockSpec(memory_space=pltpu.SMEM)
VMEM = pl.BlockSpec(memory_space=pltpu.VMEM)
HBM = pl.BlockSpec(memory_space=pltpu.HBM)
PARAMS = pltpu.CompilerParams(vmem_limit_bytes=24 * 1024 * 1024)


def route(value, target):
    pairs = []
    for i in range(BLOCKS):
        for r in range(REPLICAS):
            i2, r2 = target(i, r)
            pairs.append((i * REPLICAS + r, (i2 % BLOCKS) * REPLICAS + r2 % REPLICAS))
    return lax.ppermute(value, AXES, pairs)


def partner(i, r):
    return (i + 8, r + 1) if r % 2 == 0 else (i - 8, r - 1)


def swap_pair(value):
    return route(value, partner)


def cross_back(i, r):
    i2, r2 = partner(i, r)
    return (i2 - side(r2), r2)


def side(r):
    return 1 - 2 * (r % 2)


def offsets_of(core, pair, slot):
    return (7 * core, 1 + 5 * core, 2 + 3 * core, 3 + core)[2 * pair + slot]


def tile_steps(core_ref, mask_ref, tiles_ref, held, sems, work, present, absent):
    core = core_ref[0]
    offsets = [offsets_of(core if member == 0 else 1 - core, pair, slot) for member, pair, slot in work]

    def copy(step, t):
        return pltpu.make_async_copy(tiles_ref.at[0, t], held.at[step], sems.at[step])

    for step, t in enumerate(offsets):

        @pl.when(mask_ref[0, t] > 0)
        def _():
            copy(step, t).start()

    for step, t in enumerate(offsets):

        @pl.when(mask_ref[0, t] > 0)
        def _():
            copy(step, t).wait()
            present(step, held.at[step])

        if absent is not None:

            @pl.when(mask_ref[0, t] == 0)
            def _():
                absent(step)


def tile_scratch(count):
    return [pltpu.VMEM((count, ROWS, ROWS), BF16), pltpu.SemaphoreType.DMA((count,))]


def early_kernel(core_ref, mask_ref, tiles_ref, near, near_d, near_e, near_r, far, acc, held, sems):
    acc[...] = jnp.zeros_like(acc)
    sources = ((near, 0 * ROWS), (near_d, 0 * ROWS), (near_e, 0 * ROWS), (near_r, 0 * ROWS), (far, 0 * ROWS),)

    def present(step, tile):
        block, start = sources[step]
        acc[...] += jnp.dot(tile[...], block[start : start + ROWS, :], preferred_element_type=F32)

    tile_steps(core_ref, mask_ref, tiles_ref, held, sems, [(0, 0, 0), (1, 0, 1), (1, 0, 0), (0, 0, 1), (0, 1, 0)], present, None)


def late_kernel(core_ref, mask_ref, tiles_ref, before, far_d, far_e, far_r, keep_ref, send_ref, acc, held, sems):
    core = core_ref[0]
    acc[...] = before[...]
    sources = ((far_d, 0 * ROWS), (far_e, 0 * ROWS), (far_r, 0 * ROWS),)

    def present(step, tile):
        block, start = sources[step]
        acc[...] += jnp.dot(tile[...], block[start : start + ROWS, :], preferred_element_type=F32)

    tile_steps(core_ref, mask_ref, tiles_ref, held, sems, [(1, 1, 1), (1, 1, 0), (0, 1, 1)], present, None)
    keep_ref[...] = acc[pl.ds(pl.multiple_of(core * HALF, HALF), HALF), :]
    send_ref[...] = acc[pl.ds(pl.multiple_of(HALF - core * HALF, HALF), HALF), :].astype(send_ref.dtype)


def middle_kernel(zh_ref, parts_ref, weight_ref, grad_ref, pack_ref, full):
    wide = parts_ref[0].astype(F32)
    for s in range(1, 4):
        wide = wide + parts_ref[s].astype(F32)
    high = wide.astype(BF16)
    low = (wide - high.astype(F32)).astype(BF16)
    weight = weight_ref[...]
    total = jnp.dot(high, weight, preferred_element_type=F32) + jnp.dot(low, weight, preferred_element_type=F32)
    gate = jax.nn.sigmoid(total)
    pack_ref[:HALF] = (total * gate).astype(BF16)
    score = (grad_ref[...].astype(F32) * gate * (1.0 + total * (1.0 - gate))).astype(BF16)
    turned = lax.dot_general(weight, score, (((1,), (1,)), ((), ())), preferred_element_type=F32)
    pack_ref[HALF : 2 * HALF] = turned.astype(BF16)
    full[...] = lax.dot_general(high, score, (((0,), (0,)), ((), ())), preferred_element_type=F32)
    term = full[pl.ds(pl.multiple_of(zh_ref[0] * 64, 64), 64), :]
    term_high = term.astype(BF16)
    pack_ref[512:576] = term_high
    pack_ref[576:640] = (term - term_high.astype(F32)).astype(BF16)


def backward_kernel(plan, core_ref, mask_ref, tiles_ref, pack_ref, *rest):
    outs, held, sems = rest[: len(plan)], rest[-2], rest[-1]

    def present(step, tile):
        value = jnp.dot(pack_ref[0, HALF : 2 * HALF], tile[:HALF, :], preferred_element_type=F32)
        value = value + jnp.dot(pack_ref[1, HALF : 2 * HALF], tile[HALF:, :], preferred_element_type=F32)
        value = value.astype(BF16)
        outs[step // 2][step % 2, 0] = value[:, :HALF]
        outs[step // 2][step % 2, 1] = value[:, HALF:]

    def absent(step):
        outs[step // 2][step % 2] = jnp.zeros((2, HIDDEN, HALF), BF16)

    work = [(member, pair, slot) for member, slot in plan for pair in range(2)]
    tile_steps(core_ref, mask_ref, tiles_ref, held, sems, work, present, absent)


def turn_kernel(parts_ref, out_ref):
    wide = parts_ref[0, :HALF].astype(F32)
    for s in range(1, 4):
        wide = wide + parts_ref[s, :HALF].astype(F32)
    out_ref[:HALF] = wide.T.astype(BF16)
    for s in range(4):
        out_ref[HALF + 32 * s : HALF + 32 * (s + 1)] = parts_ref[s, HALF:]


def last_kernel(packs_ref, rows_ref, weight_ref):
    for c in range(2):
        rows_ref[c * HALF : (c + 1) * HALF] = packs_ref[c, :HALF]
        for s in range(4):
            start = HALF + 32 * s
            weight_ref[64 * s + 32 * c : 64 * s + 32 * c + 32] = packs_ref[c, start : start + 32].astype(F32)


def products(plan, core, mask, tiles, packs):
    return pl.pallas_call(
        functools.partial(backward_kernel, plan),
        out_shape=[jax.ShapeDtypeStruct((2, 2, HIDDEN, HALF), BF16) for _ in plan],
        in_specs=[SMEM, SMEM, HBM, VMEM],
        out_specs=[VMEM] * len(plan),
        scratch_shapes=tile_scratch(2 * len(plan)),
        compiler_params=PARAMS,
        cost_estimate=pl.CostEstimate(flops=2 * 10**9, bytes_accessed=6 * 2**20, transcendentals=0),
    )(core, mask, tiles, packs)


def total_of(*values):
    wide = values[0].astype(F32)
    for value in values[1:]:
        wide = wide + value.astype(F32)
    return wide


def spread_sum(value, axes):
    copies = jnp.broadcast_to(value, (8,) + value.shape)
    return jnp.sum(lax.all_to_all(copies, axes, 0, 0), axis=0)


def shards(features, weight, grad_out, tiles, tile_mask):
    core_index = lax.axis_index("c")
    core = core_index.astype(jnp.int32).reshape(1)
    zh = lax.axis_index("zh").astype(jnp.int32).reshape(1)
    even = core_index == 0
    tiles = pltpu.with_memory_space_constraint(tiles, pltpu.HBM)

    fetched1 = route(features, lambda i, r: (i + 8 * r + 2 + 3 * (r % 2), r))
    fetched0 = route(features, lambda i, r: (i + 8 * r + 7 * (r % 2), r))
    near_r = route(fetched0, lambda i, r: (i + side(r), r))
    near_e = swap_pair(fetched0)
    near_d = route(fetched0, lambda i, r: partner(i + side(r), r))
    far_r = route(fetched1, lambda i, r: (i + side(r), r))
    far_e = swap_pair(fetched1)
    far_d = route(fetched1, lambda i, r: partner(i + side(r), r))
    half = jax.ShapeDtypeStruct((HALF, HIDDEN), F32)
    half16 = jax.ShapeDtypeStruct((HALF, HIDDEN), BF16)
    before = pl.pallas_call(
        early_kernel,
        out_shape=jax.ShapeDtypeStruct((ROWS, HIDDEN), F32),
        in_specs=[SMEM, SMEM, HBM] + [VMEM] * 5,
        out_specs=VMEM,
        scratch_shapes=tile_scratch(5),
        compiler_params=PARAMS,
        cost_estimate=pl.CostEstimate(flops=2 * 10**9, bytes_accessed=6 * 2**20, transcendentals=0),
    )(core, tile_mask, tiles, fetched0, near_d, near_e, near_r, fetched1)
    keep, send = pl.pallas_call(
        late_kernel,
        out_shape=[half, half16],
        in_specs=[SMEM, SMEM, HBM] + [VMEM] * 4,
        out_specs=[VMEM, VMEM],
        scratch_shapes=[pltpu.VMEM((ROWS, HIDDEN), F32)] + tile_scratch(3),
        compiler_params=PARAMS,
    )(core, tile_mask, tiles, before, far_d, far_e, far_r)
    sent = lax.all_gather(send, "c")
    chip = (keep + jnp.where(even, sent[1], sent[0])).astype(BF16)
    parts = lax.all_gather(chip, "zh")
    grad_half = lax.dynamic_slice_in_dim(grad_out, core_index * HALF, HALF, 0)
    pack = pl.pallas_call(
        middle_kernel,
        out_shape=jax.ShapeDtypeStruct((640, HIDDEN), BF16),
        in_specs=[SMEM] + [VMEM] * 3,
        out_specs=VMEM,
        scratch_shapes=[pltpu.VMEM((HIDDEN, HIDDEN), F32)],
        compiler_params=PARAMS,
    )(zh, parts, weight, grad_half)
    packs = lax.all_gather(pack, "c")
    activated = packs[:, :HALF].reshape(ROWS, HIDDEN)

    aside, other, across, own = products(((0, 1), (1, 0), (1, 1), (0, 0)), core, tile_mask, tiles, packs)
    aside = route(aside, lambda i, r: (i - side(r), r))
    other = swap_pair(other)
    across = route(across, cross_back)
    near = total_of(own[0], aside[0], other[0], across[0]).astype(BF16)
    far = total_of(own[1], aside[1], other[1], across[1]).astype(BF16)
    home_near = route(near, lambda i, r: (i - 8 * r - 7 * (r % 2), r))
    home_far = route(far, lambda i, r: (i - 8 * r - 2 - 3 * (r % 2), r))

    high, low = packs[:, 512:576].astype(F32), packs[:, 576:640].astype(F32)
    term = lax.dynamic_slice_in_dim(high[0] + low[0] + (high[1] + low[1]), core_index * 32, 32, 0)
    term = spread_sum(term, "y")
    term, _ = lax.optimization_barrier((term, far))
    term = (spread_sum(term, ("zl", "x")) * (BLOCKS * ROWS) ** -0.5).astype(BF16)

    flipped = total_of(
        jnp.where(even, home_near[1], home_near[0]), jnp.where(even, home_far[1], home_far[0])
    ).astype(BF16)
    kept = total_of(jnp.where(even, home_near[0], home_near[1]), jnp.where(even, home_far[0], home_far[1]))
    crossed = lax.all_gather(flipped, "c")
    chip_grad = (kept + jnp.where(even, crossed[1], crossed[0])).astype(BF16)
    grad_parts = lax.all_gather(jnp.concatenate([chip_grad, term]), "zh")
    turned = pl.pallas_call(
        turn_kernel,
        out_shape=jax.ShapeDtypeStruct((HALF + 128, HIDDEN), BF16),
        in_specs=[VMEM],
        out_specs=VMEM,
        compiler_params=PARAMS,
    )(grad_parts)
    feature_grad, weight_grad = pl.pallas_call(
        last_kernel,
        out_shape=[jax.ShapeDtypeStruct((ROWS, HIDDEN), BF16), jax.ShapeDtypeStruct((HIDDEN, HIDDEN), F32)],
        in_specs=[VMEM],
        out_specs=[VMEM, VMEM],
        compiler_params=PARAMS,
    )(lax.all_gather(turned, "c"))
    return activated, feature_grad, weight_grad


def solution(mesh):
    fine = Mesh(mesh.devices.reshape(SIZES), AXES)
    nodes = P(DOM, None)
    return jax.shard_map(
        shards,
        mesh=fine,
        in_specs=(nodes, P(), nodes, P(DOM, ("zh", "c"), None, None), P(DOM, ("zh", "c"))),
        out_specs=(nodes, nodes, P()),
        check_vma=False,
    )
```

```python
import functools

import jax
import jax.numpy as jnp
from jax import lax
from jax.experimental import pallas as pl
from jax.experimental.pallas import tpu as pltpu
from jax.sharding import Mesh
from jax.sharding import PartitionSpec as P

AXES = ("zl", "x", "y", "zh", "c")
SIZES = (2, 4, 8, 4, 2)
DOM = ("zl", "x", "y")
BLOCKS = 64
REPLICAS = 8
ROWS = 512
HALF = 256
HIDDEN = 256
F32 = jnp.float32
BF16 = jnp.bfloat16
SMEM = pl.BlockSpec(memory_space=pltpu.SMEM)
VMEM = pl.BlockSpec(memory_space=pltpu.VMEM)
HBM = pl.BlockSpec(memory_space=pltpu.HBM)
PARAMS = pltpu.CompilerParams(vmem_limit_bytes=24 * 1024 * 1024)


def route(value, target):
    pairs = []
    for i in range(BLOCKS):
        for r in range(REPLICAS):
            i2, r2 = target(i, r)
            pairs.append((i * REPLICAS + r, (i2 % BLOCKS) * REPLICAS + r2 % REPLICAS))
    return lax.ppermute(value, AXES, pairs)


def partner(i, r):
    return (i + 8, r + 1) if r % 2 == 0 else (i - 8, r - 1)


def swap_pair(value):
    return route(value, partner)


def cross_back(i, r):
    i2, r2 = partner(i, r)
    return (i2 - side(r2), r2)


def side(r):
    return 1 - 2 * (r % 2)


def offsets_of(core, pair, slot):
    return (7 * core, 1 + 5 * core, 2 + 3 * core, 3 + core)[2 * pair + slot]


def tile_steps(core_ref, mask_ref, tiles_ref, held, sems, work, present, absent):
    core = core_ref[0]
    offsets = [offsets_of(core if member == 0 else 1 - core, pair, slot) for member, pair, slot in work]

    def copy(step, t):
        return pltpu.make_async_copy(tiles_ref.at[0, t], held.at[step], sems.at[step])

    for step, t in enumerate(offsets):

        @pl.when(mask_ref[0, t] > 0)
        def _():
            copy(step, t).start()

    for step, t in enumerate(offsets):

        @pl.when(mask_ref[0, t] > 0)
        def _():
            copy(step, t).wait()
            present(step, held.at[step])

        if absent is not None:

            @pl.when(mask_ref[0, t] == 0)
            def _():
                absent(step)


def tile_scratch(count):
    return [pltpu.VMEM((count, ROWS, ROWS), BF16), pltpu.SemaphoreType.DMA((count,))]


def early_kernel(core_ref, mask_ref, tiles_ref, near, near_d, near_e, near_r, far, acc, held, sems):
    acc[...] = jnp.zeros_like(acc)
    sources = ((near, 0 * ROWS), (near_d, 0 * ROWS), (near_e, 0 * ROWS), (near_r, 0 * ROWS), (far, 0 * ROWS),)

    def present(step, tile):
        block, start = sources[step]
        acc[...] += jnp.dot(tile[...], block[start : start + ROWS, :], preferred_element_type=F32)

    tile_steps(core_ref, mask_ref, tiles_ref, held, sems, [(0, 0, 0), (1, 0, 1), (1, 0, 0), (0, 0, 1), (0, 1, 0)], present, None)


def late_kernel(core_ref, mask_ref, tiles_ref, before, far_d, far_e, far_r, keep_ref, send_ref, acc, held, sems):
    core = core_ref[0]
    acc[...] = before[...]
    sources = ((far_d, 0 * ROWS), (far_e, 0 * ROWS), (far_r, 0 * ROWS),)

    def present(step, tile):
        block, start = sources[step]
        acc[...] += jnp.dot(tile[...], block[start : start + ROWS, :], preferred_element_type=F32)

    tile_steps(core_ref, mask_ref, tiles_ref, held, sems, [(1, 1, 1), (1, 1, 0), (0, 1, 1)], present, None)
    keep_ref[...] = acc[pl.ds(pl.multiple_of(core * HALF, HALF), HALF), :]
    send_ref[...] = acc[pl.ds(pl.multiple_of(HALF - core * HALF, HALF), HALF), :].astype(send_ref.dtype)


def middle_kernel(zh_ref, parts_ref, weight_ref, grad_ref, pack_ref, full):
    wide = parts_ref[0].astype(F32)
    for s in range(1, 4):
        wide = wide + parts_ref[s].astype(F32)
    high = wide.astype(BF16)
    low = (wide - high.astype(F32)).astype(BF16)
    weight = weight_ref[...]
    total = jnp.dot(high, weight, preferred_element_type=F32) + jnp.dot(low, weight, preferred_element_type=F32)
    gate = jax.nn.sigmoid(total)
    pack_ref[:HALF] = (total * gate).astype(BF16)
    score = (grad_ref[...].astype(F32) * gate * (1.0 + total * (1.0 - gate))).astype(BF16)
    turned = lax.dot_general(weight, score, (((1,), (1,)), ((), ())), preferred_element_type=F32)
    pack_ref[HALF : 2 * HALF] = turned.astype(BF16)
    full[...] = lax.dot_general(high, score, (((0,), (0,)), ((), ())), preferred_element_type=F32)
    term = full[pl.ds(pl.multiple_of(zh_ref[0] * 64, 64), 64), :]
    pack_ref[512:576] = term.astype(BF16)


def backward_kernel(plan, core_ref, mask_ref, tiles_ref, pack_ref, *rest):
    outs, held, sems = rest[: len(plan)], rest[-2], rest[-1]

    def present(step, tile):
        value = jnp.dot(pack_ref[0, HALF : 2 * HALF], tile[:HALF, :], preferred_element_type=F32)
        value = value + jnp.dot(pack_ref[1, HALF : 2 * HALF], tile[HALF:, :], preferred_element_type=F32)
        value = value.astype(BF16)
        outs[step // 2][step % 2, 0] = value[:, :HALF]
        outs[step // 2][step % 2, 1] = value[:, HALF:]

    def absent(step):
        outs[step // 2][step % 2] = jnp.zeros((2, HIDDEN, HALF), BF16)

    work = [(member, pair, slot) for member, slot in plan for pair in range(2)]
    tile_steps(core_ref, mask_ref, tiles_ref, held, sems, work, present, absent)


def turn_kernel(parts_ref, out_ref):
    wide = parts_ref[0, :HALF].astype(F32)
    for s in range(1, 4):
        wide = wide + parts_ref[s, :HALF].astype(F32)
    out_ref[:HALF] = wide.T.astype(BF16)
    for s in range(4):
        out_ref[HALF + 32 * s : HALF + 32 * (s + 1)] = parts_ref[s, HALF:]


def last_kernel(packs_ref, rows_ref, weight_ref):
    for c in range(2):
        rows_ref[c * HALF : (c + 1) * HALF] = packs_ref[c, :HALF]
        for s in range(4):
            start = HALF + 32 * s
            weight_ref[64 * s + 32 * c : 64 * s + 32 * c + 32] = packs_ref[c, start : start + 32].astype(F32)


def products(plan, core, mask, tiles, packs):
    return pl.pallas_call(
        functools.partial(backward_kernel, plan),
        out_shape=[jax.ShapeDtypeStruct((2, 2, HIDDEN, HALF), BF16) for _ in plan],
        in_specs=[SMEM, SMEM, HBM, VMEM],
        out_specs=[VMEM] * len(plan),
        scratch_shapes=tile_scratch(2 * len(plan)),
        compiler_params=PARAMS,
        cost_estimate=pl.CostEstimate(flops=2 * 10**9, bytes_accessed=6 * 2**20, transcendentals=0),
    )(core, mask, tiles, packs)


def total_of(*values):
    wide = values[0].astype(F32)
    for value in values[1:]:
        wide = wide + value.astype(F32)
    return wide


def spread_sum(value, axes):
    copies = jnp.broadcast_to(value, (8,) + value.shape)
    return jnp.sum(lax.all_to_all(copies, axes, 0, 0), axis=0)


def shards(features, weight, grad_out, tiles, tile_mask):
    core_index = lax.axis_index("c")
    core = core_index.astype(jnp.int32).reshape(1)
    zh = lax.axis_index("zh").astype(jnp.int32).reshape(1)
    even = core_index == 0
    tiles = pltpu.with_memory_space_constraint(tiles, pltpu.HBM)

    fetched1 = route(features, lambda i, r: (i + 8 * r + 2 + 3 * (r % 2), r))
    fetched0 = route(features, lambda i, r: (i + 8 * r + 7 * (r % 2), r))
    near_r = route(fetched0, lambda i, r: (i + side(r), r))
    near_e = swap_pair(fetched0)
    near_d = route(fetched0, lambda i, r: partner(i + side(r), r))
    far_r = route(fetched1, lambda i, r: (i + side(r), r))
    far_e = swap_pair(fetched1)
    far_d = route(fetched1, lambda i, r: partner(i + side(r), r))
    half = jax.ShapeDtypeStruct((HALF, HIDDEN), F32)
    half16 = jax.ShapeDtypeStruct((HALF, HIDDEN), BF16)
    before = pl.pallas_call(
        early_kernel,
        out_shape=jax.ShapeDtypeStruct((ROWS, HIDDEN), F32),
        in_specs=[SMEM, SMEM, HBM] + [VMEM] * 5,
        out_specs=VMEM,
        scratch_shapes=tile_scratch(5),
        compiler_params=PARAMS,
        cost_estimate=pl.CostEstimate(flops=2 * 10**9, bytes_accessed=6 * 2**20, transcendentals=0),
    )(core, tile_mask, tiles, fetched0, near_d, near_e, near_r, fetched1)
    keep, send = pl.pallas_call(
        late_kernel,
        out_shape=[half, half16],
        in_specs=[SMEM, SMEM, HBM] + [VMEM] * 4,
        out_specs=[VMEM, VMEM],
        scratch_shapes=[pltpu.VMEM((ROWS, HIDDEN), F32)] + tile_scratch(3),
        compiler_params=PARAMS,
    )(core, tile_mask, tiles, before, far_d, far_e, far_r)
    sent = lax.all_gather(send, "c")
    chip = (keep + jnp.where(even, sent[1], sent[0])).astype(BF16)
    parts = lax.all_gather(chip, "zh")
    grad_half = lax.dynamic_slice_in_dim(grad_out, core_index * HALF, HALF, 0)
    pack = pl.pallas_call(
        middle_kernel,
        out_shape=jax.ShapeDtypeStruct((576, HIDDEN), BF16),
        in_specs=[SMEM] + [VMEM] * 3,
        out_specs=VMEM,
        scratch_shapes=[pltpu.VMEM((HIDDEN, HIDDEN), F32)],
        compiler_params=PARAMS,
    )(zh, parts, weight, grad_half)
    packs = lax.all_gather(pack, "c")
    activated = packs[:, :HALF].reshape(ROWS, HIDDEN)

    aside, other, across, own = products(((0, 1), (1, 0), (1, 1), (0, 0)), core, tile_mask, tiles, packs)
    aside = route(aside, lambda i, r: (i - side(r), r))
    other = swap_pair(other)
    across = route(across, cross_back)
    near = total_of(own[0], aside[0], other[0], across[0]).astype(BF16)
    far = total_of(own[1], aside[1], other[1], across[1]).astype(BF16)
    home_near = route(near, lambda i, r: (i - 8 * r - 7 * (r % 2), r))
    home_far = route(far, lambda i, r: (i - 8 * r - 2 - 3 * (r % 2), r))

    terms = packs[:, 512:576].astype(F32)
    term = lax.dynamic_slice_in_dim(terms[0] + terms[1], core_index * 32, 32, 0)
    term = spread_sum(term, "y")
    term, _ = lax.optimization_barrier((term, far))
    term = (spread_sum(term, ("zl", "x")) * (BLOCKS * ROWS) ** -0.5).astype(BF16)

    flipped = total_of(
        jnp.where(even, home_near[1], home_near[0]), jnp.where(even, home_far[1], home_far[0])
    ).astype(BF16)
    kept = total_of(jnp.where(even, home_near[0], home_near[1]), jnp.where(even, home_far[0], home_far[1]))
    crossed = lax.all_gather(flipped, "c")
    chip_grad = (kept + jnp.where(even, crossed[1], crossed[0])).astype(BF16)
    grad_parts = lax.all_gather(jnp.concatenate([chip_grad, term]), "zh")
    turned = pl.pallas_call(
        turn_kernel,
        out_shape=jax.ShapeDtypeStruct((HALF + 128, HIDDEN), BF16),
        in_specs=[VMEM],
        out_specs=VMEM,
        compiler_params=PARAMS,
    )(grad_parts)
    feature_grad, weight_grad = pl.pallas_call(
        last_kernel,
        out_shape=[jax.ShapeDtypeStruct((ROWS, HIDDEN), BF16), jax.ShapeDtypeStruct((HIDDEN, HIDDEN), F32)],
        in_specs=[VMEM],
        out_specs=[VMEM, VMEM],
        compiler_params=PARAMS,
    )(lax.all_gather(turned, "c"))
    return activated, feature_grad, weight_grad


def solution(mesh):
    fine = Mesh(mesh.devices.reshape(SIZES), AXES)
    nodes = P(DOM, None)
    return jax.shard_map(
        shards,
        mesh=fine,
        in_specs=(nodes, P(), nodes, P(DOM, ("zh", "c"), None, None), P(DOM, ("zh", "c"))),
        out_specs=(nodes, nodes, P()),
        check_vma=False,
    )
```
